256 devices in a mesh: pair: 32 (over y, z_lo, core), virt: 8 (over x, z_hi).
Axes of the slice: x: 4, y: 4, z: 8 (z_hi: 2, z_lo: 4; z = z_hi * 4 + z_lo), core: 2. Of those that a mesh axis runs over, the one named last changes fastest.
Arguments:
- amplitudes: bfloat16 [24576, 1024], P('pair'), may hold values from -24 to 24
- integrals: bfloat16 [1024, 8, 4096], P('pair', 'virt'), may hold values from -0.1875 to 0.1875
- pair_irrep: int32 [384], P('pair'), may hold values from 0 to 7
- cd_irrep: int32 [16], replicated, may hold values from 0 to 7, as said below
- mirror_tile: int32 [384], P('pair'), may hold values from 0 to 383, as said below
- pair_energy: float32 [24576], P('pair'), may hold values from -3 to -1
- virt_energy: float32 [8, 64], P('virt'), may hold values from 0.5 to 3
Outputs:
- update: bfloat16 [24576, 8, 4096], P('pair', 'virt')
The draws below stay inside these ranges and needn't reach their ends.
Inputs may be any that keep to these rules, and one draw needn't show every extreme that they name: `mirror_tile`: the partner of a tile held on pair index p is held on pair index p + 32 / 2 modulo 32; the partner's partner is the tile itself. `cd_irrep`: when 16 >= 8 every label 0 to 7 is given to some block.
All inputs are finite; a program needn't handle non-finite values.
Results may differ from the reference program's by a relative error of at most 0.001.
Values may be sent and summed in bfloat16 or wider, within the bound.
No kernel may reach another device: no remote copies, remote signals or barrier semaphores. Data moves between devices by JAX's collectives and lax.ppermute only.
A program may use at most 128 MiB of HBM per device.

```python
import math
import jax
import jax.numpy as jnp
from jax import lax

TP = 64
VW = 64
CD_WIDTH = 64
CD_BLOCKS = 16
TILES_DEV = 12
TILES = 384
PAIRS = 24576
CD = 1024
VTILES = 8
N_PAIR = 32


def draw_cd_irrep(key, part):
    key = jax.random.fold_in(key, 3)
    first, second = jax.random.split(key)
    order = jax.random.permutation(first, 8).astype(jnp.int32)
    spread = jax.random.randint(second, (CD_BLOCKS,), 0, 8).astype(jnp.int32)
    index = jnp.arange(CD_BLOCKS, dtype=jnp.int32)
    return jnp.where(index < 8, order[index % 8], spread).astype(jnp.int32)


def draw_mirror_tile(key, part):
    key = jax.random.fold_in(key, 5)
    half = N_PAIR // 2
    keys = jax.random.split(key, half)
    perms = jax.vmap(lambda single: jax.random.permutation(single, TILES_DEV))(keys).astype(jnp.int32)
    inverse = jnp.argsort(perms, axis=1).astype(jnp.int32)
    owners = jnp.arange(half, dtype=jnp.int32)[:, None]
    lower = (owners + half) * TILES_DEV + perms
    upper = owners * TILES_DEV + inverse
    return jnp.concatenate([lower, upper], 0).reshape(-1).astype(jnp.int32)


def plant(entries, key, low, high):
    shape = entries.shape
    index_at = [jax.random.randint(jax.random.fold_in(key, axis), (), 0, shape[axis]) for axis in range(len(shape))]
    entries = entries.at[tuple(index_at)].set(low)
    longest = shape.index(max(shape))
    index_at[longest] = (index_at[longest] + 1) % shape[longest]
    return entries.at[tuple(index_at)].set(high)


def block_scale(own_key, extent, cuts, low, largest):
    def one(position, blocks):
        heights = jax.random.uniform(jax.random.fold_in(jax.random.fold_in(own_key, 6), position), (blocks,), jnp.float32, low / len(cuts), largest / len(cuts))
        return jnp.repeat(jnp.exp(heights), extent[position] // blocks).reshape((-1,) + (1,) * (len(extent) - position - 1))

    loudness = one(*cuts[0])
    for cut in cuts[1:]:
        loudness = loudness * one(*cut)
    return loudness


def bell_draw(own_key, extent, width, bound, cuts=(), kind=jnp.bfloat16):
    loudness = block_scale(own_key, extent, cuts, -0.22, 0.18) if cuts else 1.0
    entries = jax.random.normal(own_key, extent, jnp.float32) * width * loudness
    return jnp.minimum(jnp.maximum(entries, -bound), bound).astype(kind)


def setup_inputs(seed: int = 0) -> dict:
    splits = jax.random.split(jax.random.key(seed), 8)
    amplitudes = bell_draw(splits[0], (PAIRS, CD), 4.0, 24.0, ((0, 32),))
    integrals = bell_draw(splits[1], (CD, VTILES, VW * VW), CD ** -0.5, 0.1875, ((0, 32), (1, 8)))
    pair_irrep = plant(jax.random.randint(splits[2], (TILES,), 0, 8), jax.random.fold_in(splits[2], 1), 0, 7).astype(jnp.int32)
    cd_irrep = draw_cd_irrep(jax.random.fold_in(splits[7], 71), 0)
    mirror_tile = draw_mirror_tile(jax.random.fold_in(splits[7], 71), 0)
    pair_energy = jnp.clip(-3.0 + 2.0 * jax.random.uniform(splits[5], (PAIRS,), jnp.float32) ** block_scale(splits[5], (PAIRS,), ((0, 32),), -0.2, 0.2), -3.0, -1.0)
    virt_energy = jnp.clip(jnp.exp(math.log(3.0) - 1.7917595 * jax.random.uniform(splits[6], (VTILES, VW), jnp.float32) ** block_scale(splits[6], (VTILES, VW), ((0, 8),), -0.2, 0.2)), 0.5, 3.0)
    return dict(amplitudes=amplitudes, integrals=integrals, pair_irrep=pair_irrep, cd_irrep=cd_irrep, mirror_tile=mirror_tile, pair_energy=pair_energy, virt_energy=virt_energy)


def reference(amplitudes, integrals, pair_irrep, cd_irrep, mirror_tile, pair_energy, virt_energy):
    live = (pair_irrep[:, None] == cd_irrep[None, :]).astype(amplitudes.dtype)
    masked = (amplitudes.reshape(TILES, TP, CD_BLOCKS, CD_WIDTH) * live[:, None, :, None]).reshape(TILES * TP, CD)
    partner_rows = (mirror_tile[:, None] * TP + jnp.arange(TP, dtype=jnp.int32)[None, :]).reshape(-1).astype(jnp.int32)
    mirrored = masked[partner_rows]

    def one_tile(operands):
        block, energy = operands
        direct = jnp.dot(masked, block, preferred_element_type=jnp.float32)
        other = jnp.dot(mirrored, block, preferred_element_type=jnp.float32)
        other = other.reshape(-1, VW, VW).transpose(0, 2, 1).reshape(-1, VW * VW)
        pair_sum = (energy[:, None] + energy[None, :]).reshape(-1)
        return ((direct + other) / (pair_sum[None, :] - pair_energy[:, None])).astype(jnp.bfloat16)

    result = lax.map(one_tile, (jnp.moveaxis(integrals, 1, 0), virt_energy))
    return jnp.moveaxis(result, 0, 1)
```

```python
import functools
import jax
import jax.numpy as jnp
import numpy as np
from jax import lax
from jax.experimental import pallas as pl
from jax.experimental.pallas import tpu as pltpu
from jax.sharding import PartitionSpec as P

BF = jnp.bfloat16
F32 = jnp.float32
I32 = jnp.int32
NT = (((1,), (1,)), ((), ()))
MIB = 1 << 20
SLOTS = 4
SPILL = 6
WIDE = 128


def place(y, z, core):
    return (y % 4) * 8 + z * 2 + core


def pairs_of(first, second):
    pairs = []
    for y in range(4):
        for z in range(4):
            for core, hop in enumerate((first, second)):
                if hop is not None:
                    pairs.append((place(y, z, core), place(*hop(y, z), core)))
    return pairs


def along_y(step):
    return lambda y, z: (y + step, z)


def along_z(flip):
    return lambda y, z: (y, z ^ flip)


def send(array, first, second):
    return lax.ppermute(array, "pair", pairs_of(first, second))


def swap_cores(array):
    return lax.ppermute(array, "pair", [(i, i ^ 1) for i in range(32)])


def order_table():
    table = np.zeros((32, 32), np.int32)
    for y in range(4):
        for z in range(4):
            for core in range(2):
                groups = []
                for chunk in range(4):
                    for side in (core, 1 - core):
                        one = {
                            1: ((y - 1, z), (y + 1, z)),
                            2: ((y, z ^ 1), (y, z ^ 2)),
                            3: ((y, z ^ 3), (y + 2, z)),
                            4: ((y - 1, z ^ 1), (y - 1, z ^ 2)),
                            5: ((y + 1, z ^ 1), (y + 1, z ^ 2)),
                            6: ((y - 1, z ^ 3), (y + 2, z ^ 1)),
                            7: ((y + 1, z ^ 3), (y + 2, z ^ 2)),
                        }
                        for piece in ((1, 2), (3, 4), (5, 6), (7,))[chunk]:
                            spot = one[piece][side]
                            groups += [place(*spot, 0), place(*spot, 1)]
                        if chunk == 3:
                            groups += [place(y, z, side), place(y + 2, z ^ 3, side)]
                table[place(y, z, core)] = groups
    return table


def params(mib):
    return pltpu.CompilerParams(vmem_limit_bytes=mib * MIB)


def cost(flops, bytes_accessed):
    return pl.CostEstimate(flops=flops, bytes_accessed=bytes_accessed, transcendentals=0)


SMEM = pl.BlockSpec(memory_space=pltpu.SMEM)
VMEM = pl.BlockSpec(memory_space=pltpu.VMEM)


def join_kernel(core_ref, own, other, out):
    core = core_ref[0]
    out[pl.ds(pl.multiple_of(core * 32, 32), 32), :] = own[...]
    out[pl.ds(pl.multiple_of(32 - core * 32, 32), 32), :] = other[...]


def join_cores(core, own, other):
    rows, columns = own.shape
    return pl.pallas_call(
        join_kernel,
        in_specs=[SMEM, VMEM, VMEM],
        out_specs=VMEM,
        out_shape=jax.ShapeDtypeStruct((2 * rows, columns), BF),
        compiler_params=params(8),
        cost_estimate=cost(0, 4 * rows * columns * 2),
    )(core, own, other)


def ranks_of(labels, blocks):
    ranks = []
    for b in range(blocks):
        rank = jnp.int32(0)
        for earlier in range(b):
            rank += (labels[earlier] == labels[b]).astype(I32)
        ranks.append(rank)
    return ranks


def spread(shape, axis, width, scalars):
    group = lax.broadcasted_iota(I32, shape, axis) // width
    out = jnp.full(shape, -1, I32)
    for i, scalar in enumerate(scalars):
        out = jnp.where(group == i, scalar, out)
    return out


def compact_kernel(first, slots, cd, irreps, amplitudes, out, masked):
    blocks = cd.shape[0]
    tiles = irreps.shape[0]
    rows, width = amplitudes.shape
    tile = rows // tiles
    block = width // blocks
    ranks = ranks_of(cd, blocks)
    label_row = spread((1, width), 1, block, [cd[b] for b in range(blocks)])
    for t in range(tiles):
        live = (label_row == irreps[t]).astype(F32).astype(BF)
        masked[t * tile : (t + 1) * tile, :] = amplitudes[t * tile : (t + 1) * tile, :] * live
    for half in range(slots * block // WIDE):
        column = lax.broadcasted_iota(I32, (block, WIDE), 1) + half * WIDE
        inner = lax.broadcasted_iota(I32, (block, WIDE), 0)
        choose = []
        for b in range(blocks):
            want = (ranks[b] - first) * block + inner
            choose.append((column == want).astype(F32).astype(BF))
        picked = jnp.dot(masked[...], jnp.concatenate(choose, 0), preferred_element_type=F32)
        out[:, half * WIDE : (half + 1) * WIDE] = picked.astype(BF)


def compact(first, slots, cd, irreps, amplitudes):
    rows, width = amplitudes.shape
    block = width // cd.shape[0]
    return pl.pallas_call(
        functools.partial(compact_kernel, first, slots),
        in_specs=[SMEM, SMEM, VMEM],
        out_specs=VMEM,
        out_shape=jax.ShapeDtypeStruct((rows, slots * block), BF),
        scratch_shapes=[pltpu.VMEM((rows, width), BF)],
        compiler_params=params(24),
        cost_estimate=cost(2 * rows * width * slots * block, rows * width * 2),
    )(cd, irreps, amplitudes)


def left_kernel(cd, irreps, there, mirror, order, amplitudes, sent, spill, direct, crossed, rowed, rowed_spill):
    blocks = cd.shape[0]
    tiles = irreps.shape[0]
    rows, width = amplitudes.shape
    tile = rows // tiles
    block = width // blocks
    groups = order.shape[0]
    group = width // groups
    per = block // group
    ranks = ranks_of(cd, blocks)
    most = ranks[0]
    for rank in ranks[1:]:
        most = jnp.maximum(most, rank)
    sources = [lax.rem(mirror[t], tiles) for t in range(tiles)]
    for t in range(tiles):
        rows_t = pl.ds(pl.multiple_of(sources[t] * tile, tile), tile)
        rowed[t * tile : (t + 1) * tile, :] = sent[rows_t, :]

    @pl.when(most >= SLOTS)
    def _():
        for t in range(tiles):
            rows_t = pl.ds(pl.multiple_of(sources[t] * tile, tile), tile)
            rowed_spill[t * tile : (t + 1) * tile, :] = spill[rows_t, :]

    here = 256
    for part in range(width // here):
        mine = [order[part * (here // group) + i] for i in range(here // group)]
        lane = lax.broadcasted_iota(I32, (1, here), 1) % group
        origin = spread((1, here), 1, group, [owner * group for owner in mine]) + lane
        labels = spread((1, here), 1, group, [cd[owner // per] for owner in mine])
        rank_row = spread((1, here), 1, group, [rank_at(ranks, owner // per) for owner in mine])
        columns = slice(part * here, (part + 1) * here)
        pick = (lax.broadcasted_iota(I32, (width, here), 0) == origin).astype(F32).astype(BF)
        moved = jnp.dot(amplitudes[...], pick, preferred_element_type=F32)
        slot = rank_row * block + origin % block
        pick = (lax.broadcasted_iota(I32, (SLOTS * block, here), 0) == slot).astype(F32).astype(BF)
        opened = jnp.dot(rowed[...], pick, preferred_element_type=F32)
        for t in range(tiles):
            at = slice(t * tile, (t + 1) * tile)
            direct[at, columns] = jnp.where(labels == irreps[t], moved[at], 0.0).astype(BF)
            crossed[at, columns] = jnp.where(labels == there[sources[t]], opened[at], 0.0).astype(BF)

        @pl.when(most >= SLOTS)
        def _():
            late = slot - SLOTS * block
            choose = (lax.broadcasted_iota(I32, (SPILL * block, here), 0) == late).astype(F32).astype(BF)
            rest = jnp.dot(rowed_spill[...], choose, preferred_element_type=F32)
            for t in range(tiles):
                at = slice(t * tile, (t + 1) * tile)
                crossed[at, columns] += jnp.where(labels == there[sources[t]], rest[at], 0.0).astype(BF)


def rank_at(ranks, index):
    out = jnp.int32(0)
    for b, rank in enumerate(ranks):
        out = jnp.where(index == b, rank, out)
    return out


def left_sides(cd, irreps, there, mirror, order, amplitudes, sent, spill):
    rows, width = amplitudes.shape
    shape = jax.ShapeDtypeStruct((rows, width), BF)
    return pl.pallas_call(
        left_kernel,
        in_specs=[SMEM] * 5 + [VMEM] * 3,
        out_specs=[VMEM, VMEM],
        out_shape=[shape, shape],
        scratch_shapes=[pltpu.VMEM(sent.shape, BF), pltpu.VMEM(spill.shape, BF)],
        compiler_params=params(40),
        cost_estimate=cost(2 * rows * width * (width + sent.shape[1]), rows * width * 6),
    )(cd, irreps, there, mirror, order, amplitudes, sent, spill)


def turn_kernel(edge, steps, *refs):
    pieces, out, held = refs[:-2], refs[-2], refs[-1]
    step = pl.program_id(0)
    wide = edge * edge // steps

    @pl.when(step < steps)
    def _():
        at = pl.multiple_of(step * wide, wide)
        for i in range(wide // WIDE):
            columns = slice(i * WIDE, (i + 1) * WIDE)
            block = jnp.concatenate([piece[:, columns] for piece in pieces], 0)
            turned = block.T
            out[0, columns, :] = turned
            held[pl.ds(pl.multiple_of(at + i * WIDE, WIDE), WIDE), :] = turned.astype(F32)

    @pl.when(step >= steps)
    def _():
        some = edge // steps
        at = pl.multiple_of((step - steps) * some, some)
        for low in range(0, some, 8):
            parts = []
            for b in range(0, edge, 8):
                rows = [held[pl.ds(pl.multiple_of((b + i) * edge + at + low, 8), 8), :] for i in range(8)]
                parts.append(jnp.swapaxes(jnp.stack(rows, 0), 0, 1))
            whole = jnp.concatenate(parts, 1)
            out[0, low * edge : (low + 8) * edge, :] = whole.reshape(8 * edge, WIDE).astype(BF)


def turn(edge, *pieces):
    steps = 4
    columns = edge * edge
    wide = columns // steps
    return pl.pallas_call(
        functools.partial(turn_kernel, edge, steps),
        grid=(2 * steps,),
        in_specs=[pl.BlockSpec((p.shape[0], wide), lambda g: (0, jnp.minimum(g, steps - 1))) for p in pieces],
        out_specs=pl.BlockSpec((1, wide, WIDE), lambda g: (g // steps, lax.rem(g, steps), 0)),
        out_shape=jax.ShapeDtypeStruct((2, columns, WIDE), BF),
        scratch_shapes=[pltpu.VMEM((columns, WIDE), F32)],
        compiler_params=params(24),
        cost_estimate=cost(columns * WIDE * 2, columns * WIDE * 6),
    )(*pieces)


def ladder_kernel(chunks, last, *refs):
    direct, crossed = refs[:2]
    sides = refs[2 : 2 + 2 * chunks]
    rest = refs[2 + 2 * chunks :]
    left = jnp.concatenate([direct[...], crossed[...]], 1)
    right = jnp.concatenate([s[0] for s in sides] + [s[1] for s in sides], 1)
    total = lax.dot_general(left, right, NT, preferred_element_type=F32)
    if not last:
        rest[0][...] = total
        return
    held, row_energy, column_energy, out, spread_energy = rest
    rows = total.shape[0]

    @pl.when(pl.program_id(0) == 0)
    def _():
        for i in range(rows // WIDE):
            at = slice(i * WIDE, (i + 1) * WIDE)
            spread_energy[at, :] = jnp.broadcast_to(row_energy[:, at], (WIDE, WIDE)).T

    for i in range(total.shape[1] // WIDE):
        at = slice(i * WIDE, (i + 1) * WIDE)
        denominator = column_energy[:, at] - spread_energy[...]
        out[:, at] = ((total[:, at] + held[:, at]) / denominator).astype(BF)


def ladder(which, chunks, direct, crossed, sides, held=None, row_energy=None, column_energy=None):
    last = held is not None
    rows = direct.shape[0]
    columns = sides[0].shape[1]
    wide = 512
    depth = chunks * 2 * WIDE
    left = pl.BlockSpec((rows, depth), lambda g: (0, which))
    right = pl.BlockSpec((2, wide, WIDE), lambda g: (0, g, 0))
    block = pl.BlockSpec((rows, wide), lambda g: (0, g))
    in_specs = [left, left] + [right] * (2 * chunks)
    args = [direct, crossed, *sides]
    scratch = []
    if last:
        in_specs += [block, pl.BlockSpec((1, rows), lambda g: (0, 0)), pl.BlockSpec((1, wide), lambda g: (0, g))]
        args += [held, row_energy, column_energy]
        scratch = [pltpu.VMEM((rows, WIDE), F32)]
    return pl.pallas_call(
        functools.partial(ladder_kernel, chunks, last),
        grid=(columns // wide,),
        in_specs=in_specs,
        out_specs=block,
        out_shape=jax.ShapeDtypeStruct((rows, columns), BF if last else F32),
        scratch_shapes=scratch,
        compiler_params=params(48),
        cost_estimate=cost(2 * rows * columns * 2 * depth, rows * columns * 6),
    )(*args)


def body(amplitudes, integrals, pair_irrep, cd_irrep, mirror_tile, pair_energy, virt_energy):
    rows = amplitudes.shape[0]
    edge = virt_energy.shape[1]
    columns = edge * edge
    me = lax.axis_index("pair")
    core = (me % 2).astype(I32)
    own = integrals.reshape(integrals.shape[0], columns)

    sent = send(compact(0, SLOTS, cd_irrep, pair_irrep, amplitudes), along_y(2), along_y(2))
    there = send(pair_irrep, along_y(2), along_y(2))
    same = (cd_irrep[:, None] == cd_irrep[None, :]).sum(1)

    def more():
        return send(compact(SLOTS, SPILL, cd_irrep, pair_irrep, amplitudes), along_y(2), along_y(2))

    def none():
        return jnp.zeros((rows, SPILL * edge), BF)

    spill = lax.cond(same.max() > SLOTS, more, none)

    block = join_cores(core.reshape(1), own, swap_cores(own))
    p1 = send(block, along_y(1), along_y(-1))
    p2 = send(block, along_z(1), along_z(2))
    p3 = send(block, along_z(3), along_y(2))
    p4 = send(p2, along_y(1), along_y(1))
    p5 = send(p2, along_y(-1), along_y(-1))
    p6 = send(p3, along_y(1), along_z(1))
    p7 = send(p3, along_y(-1), along_z(2))
    half = lax.dynamic_slice(p3, (core * 32, jnp.int32(0)), (32, columns))
    p8 = send(half, along_y(2), along_z(3))

    order = jnp.asarray(order_table())[me]
    direct, crossed = left_sides(cd_irrep, pair_irrep, there, mirror_tile, order, amplitudes, sent, spill)

    sides = []
    for pieces in ((p1, p2), (p3, p4), (p5, p6), (p7, own, p8)):
        mine = turn(edge, *pieces)
        sides.append([mine, swap_cores(mine)])

    column_energy = (virt_energy[0][:, None] + virt_energy[0][None, :]).reshape(1, columns)
    row_energy = pair_energy.reshape(1, rows)
    held = ladder(0, 2, direct, crossed, sides[0] + sides[1])
    out = ladder(1, 2, direct, crossed, sides[2] + sides[3], held, row_energy, column_energy)
    return out.reshape(rows, 1, columns)


def solution(mesh):
    placed = (
        P("pair", None),
        P("pair", "virt", None),
        P("pair"),
        P(),
        P("pair"),
        P("pair"),
        P("virt", None),
    )
    return jax.shard_map(
        body, mesh=mesh, in_specs=placed, out_specs=P("pair", "virt", None), check_vma=False
    )
```

```python
import functools
import jax
import jax.numpy as jnp
import numpy as np
from jax import lax
from jax.experimental import pallas as pl
from jax.experimental.pallas import tpu as pltpu
from jax.sharding import PartitionSpec as P

BF = jnp.bfloat16
F32 = jnp.float32
I32 = jnp.int32
NT = (((1,), (1,)), ((), ()))
MIB = 1 << 20
SLOTS = 4
SPILL = 6
WIDE = 128


def place(y, z, core):
    return (y % 4) * 8 + z * 2 + core


def pairs_of(first, second):
    pairs = []
    for y in range(4):
        for z in range(4):
            for core, hop in enumerate((first, second)):
                if hop is not None:
                    pairs.append((place(y, z, core), place(*hop(y, z), core)))
    return pairs


def along_y(step):
    return lambda y, z: (y + step, z)


def along_z(flip):
    return lambda y, z: (y, z ^ flip)


def send(array, first, second):
    return lax.ppermute(array, "pair", pairs_of(first, second))


def swap_cores(array):
    return lax.ppermute(array, "pair", [(i, i ^ 1) for i in range(32)])


def order_table():
    table = np.zeros((32, 32), np.int32)
    for y in range(4):
        for z in range(4):
            for core in range(2):
                groups = []
                for chunk in range(4):
                    for side in (core, 1 - core):
                        one = {
                            1: ((y - 1, z), (y + 1, z)),
                            2: ((y, z ^ 1), (y, z ^ 2)),
                            3: ((y, z ^ 3), (y + 2, z)),
                            4: ((y - 1, z ^ 1), (y - 1, z ^ 2)),
                            5: ((y + 1, z ^ 1), (y + 1, z ^ 2)),
                            6: ((y - 1, z ^ 3), (y + 2, z ^ 1)),
                            7: ((y + 1, z ^ 3), (y + 2, z ^ 2)),
                        }
                        for piece in ((1, 2), (3, 4), (5, 6), (7,))[chunk]:
                            spot = one[piece][side]
                            groups += [place(*spot, 0), place(*spot, 1)]
                        if chunk == 3:
                            groups += [place(y, z, side), place(y + 2, z ^ 3, side)]
                table[place(y, z, core)] = groups
    return table


def params(mib):
    return pltpu.CompilerParams(vmem_limit_bytes=mib * MIB)


def cost(flops, bytes_accessed):
    return pl.CostEstimate(flops=0, bytes_accessed=0, transcendentals=0)


SMEM = pl.BlockSpec(memory_space=pltpu.SMEM)
VMEM = pl.BlockSpec(memory_space=pltpu.VMEM)
ANY = pl.BlockSpec(memory_space=pl.ANY)
LABELS = 16


def join_kernel(core_ref, own, other, after, out):
    core = core_ref[0]
    out[pl.ds(pl.multiple_of(core * 32, 32), 32), :] = own[...]
    out[pl.ds(pl.multiple_of(32 - core * 32, 32), 32), :] = other[...]


def join_cores(core, own, other, after):
    rows, columns = own.shape
    return pl.pallas_call(
        join_kernel,
        in_specs=[SMEM, VMEM, VMEM, ANY],
        out_specs=VMEM,
        out_shape=jax.ShapeDtypeStruct((2 * rows, columns), BF),
        compiler_params=params(8),
        cost_estimate=cost(0, 4 * rows * columns * 2),
    )(core, own, other, after)


def ranks_of(labels, blocks):
    ranks = []
    for b in range(blocks):
        rank = jnp.int32(0)
        for earlier in range(b):
            rank += (labels[earlier] == labels[b]).astype(I32)
        ranks.append(rank)
    return ranks


def spread(shape, axis, width, scalars):
    group = lax.broadcasted_iota(I32, shape, axis) // width
    out = jnp.full(shape, -1, I32)
    for i, scalar in enumerate(scalars):
        out = jnp.where(group == i, scalar, out)
    return out


def compact_kernel(first, slots, cd, irreps, amplitudes, out, masked):
    blocks = cd.shape[0]
    tiles = irreps.shape[0]
    rows, width = amplitudes.shape
    tile = rows // tiles
    block = width // blocks
    ranks = ranks_of(cd, blocks)
    label_row = spread((1, width), 1, block, [cd[b] for b in range(blocks)])
    for t in range(tiles):
        live = (label_row == irreps[t]).astype(F32).astype(BF)
        masked[t * tile : (t + 1) * tile, :] = amplitudes[t * tile : (t + 1) * tile, :] * live
    for half in range(slots * block // WIDE):
        column = lax.broadcasted_iota(I32, (block, WIDE), 1) + half * WIDE
        inner = lax.broadcasted_iota(I32, (block, WIDE), 0)
        choose = []
        for b in range(blocks):
            want = (ranks[b] - first) * block + inner
            choose.append((column == want).astype(F32).astype(BF))
        picked = jnp.dot(masked[...], jnp.concatenate(choose, 0), preferred_element_type=F32)
        out[:rows, half * WIDE : (half + 1) * WIDE] = picked.astype(BF)
    tags = spread((LABELS, slots * block), 0, 1, [irreps[t] for t in range(tiles)])
    out[rows:, :] = tags.astype(F32).astype(BF)


def compact(first, slots, cd, irreps, amplitudes):
    rows, width = amplitudes.shape
    block = width // cd.shape[0]
    return pl.pallas_call(
        functools.partial(compact_kernel, first, slots),
        in_specs=[SMEM, SMEM, VMEM],
        out_specs=VMEM,
        out_shape=jax.ShapeDtypeStruct((rows + LABELS, slots * block), BF),
        scratch_shapes=[pltpu.VMEM((rows, width), BF)],
        compiler_params=params(24),
        cost_estimate=cost(2 * rows * width * slots * block, rows * width * 2),
    )(cd, irreps, amplitudes)


def left_kernel(cd, irreps, mirror, order, amplitudes, sent, spill, out, rowed, rowed_spill):
    blocks = cd.shape[0]
    tiles = irreps.shape[0]
    rows, width = amplitudes.shape
    tile = rows // tiles
    block = width // blocks
    groups = order.shape[0]
    group = width // groups
    per = block // group
    ranks = ranks_of(cd, blocks)
    most = ranks[0]
    for rank in ranks[1:]:
        most = jnp.maximum(most, rank)
    sources = [lax.rem(mirror[t], tiles) for t in range(tiles)]
    for t in range(tiles):
        rows_t = pl.ds(pl.multiple_of(sources[t] * tile, tile), tile)
        rowed[t * tile : (t + 1) * tile, :] = sent[rows_t, :]

    @pl.when(most >= SLOTS)
    def _():
        for t in range(tiles):
            rows_t = pl.ds(pl.multiple_of(sources[t] * tile, tile), tile)
            rowed_spill[t * tile : (t + 1) * tile, :] = spill[rows_t, :]

    here = 2 * WIDE
    tags = sent[rows:, :].astype(F32)
    row = lax.broadcasted_iota(I32, tags.shape, 0)
    theirs = [jnp.where(row == sources[t], tags, 0.0).sum(0, keepdims=True) for t in range(tiles)]
    for part in range(width // here):
        mine = [order[part * (here // group) + i] for i in range(here // group)]
        lane = lax.broadcasted_iota(I32, (1, here), 1) % group
        origin = spread((1, here), 1, group, [owner * group for owner in mine]) + lane
        labels = spread((1, here), 1, group, [cd[owner // per] for owner in mine])
        rank_row = spread((1, here), 1, group, [rank_at(ranks, owner // per) for owner in mine])
        pick = (lax.broadcasted_iota(I32, (width, here), 0) == origin).astype(F32).astype(BF)
        moved = jnp.dot(amplitudes[...], pick, preferred_element_type=F32)
        slot = rank_row * block + origin % block
        pick = (lax.broadcasted_iota(I32, (SLOTS * block, here), 0) == slot).astype(F32).astype(BF)
        opened = jnp.dot(rowed[...], pick, preferred_element_type=F32)
        wanted = labels.astype(F32)
        for t in range(tiles):
            at = slice(t * tile, (t + 1) * tile)
            straight = jnp.where(labels == irreps[t], moved[at], 0.0).astype(BF)
            mirrored = jnp.where(wanted == theirs[t], opened[at], 0.0).astype(BF)
            for side in range(2):
                lanes = slice(side * WIDE, (side + 1) * WIDE)
                start = (4 * part + 2 * side) * WIDE
                out[at, start : start + WIDE] = straight[:, lanes]
                out[at, start + WIDE : start + 2 * WIDE] = mirrored[:, lanes]

        @pl.when(most >= SLOTS)
        def _():
            late = slot - SLOTS * block
            choose = (lax.broadcasted_iota(I32, (SPILL * block, here), 0) == late).astype(F32).astype(BF)
            rest = jnp.dot(rowed_spill[...], choose, preferred_element_type=F32)
            for t in range(tiles):
                at = slice(t * tile, (t + 1) * tile)
                mirrored = jnp.where(wanted == theirs[t], rest[at], 0.0).astype(BF)
                for side in range(2):
                    start = (4 * part + 2 * side + 1) * WIDE
                    out[at, start : start + WIDE] += mirrored[:, side * WIDE : (side + 1) * WIDE]


def rank_at(ranks, index):
    out = jnp.int32(0)
    for b, rank in enumerate(ranks):
        out = jnp.where(index == b, rank, out)
    return out


def left_sides(cd, irreps, mirror, order, amplitudes, sent, spill):
    rows, width = amplitudes.shape
    return pl.pallas_call(
        left_kernel,
        in_specs=[SMEM] * 4 + [VMEM] * 3,
        out_specs=VMEM,
        out_shape=jax.ShapeDtypeStruct((rows, 2 * width), BF),
        scratch_shapes=[pltpu.VMEM((rows, sent.shape[1]), BF), pltpu.VMEM((rows, spill.shape[1]), BF)],
        compiler_params=params(32),
        cost_estimate=cost(2 * rows * width * (width + sent.shape[1]), rows * width * 6),
    )(cd, irreps, mirror, order, amplitudes, sent, spill)


def turn_kernel(edge, count, *refs):
    pieces, out, held = refs[:count], refs[-2], refs[-1]
    for i in range(edge * edge // WIDE):
        columns = slice(i * WIDE, (i + 1) * WIDE)
        turned = jnp.concatenate([piece[:, columns] for piece in pieces], 0).T
        out[columns, :WIDE] = turned
        held[columns, :] = turned.astype(F32)
    for low in range(0, edge, 8):
        parts = []
        for b in range(0, edge, 8):
            rows = [held[(b + i) * edge + low : (b + i) * edge + low + 8, :] for i in range(8)]
            parts.append(jnp.swapaxes(jnp.stack(rows, 0), 0, 1))
        whole = jnp.concatenate(parts, 1)
        out[low * edge : (low + 8) * edge, WIDE:] = whole.reshape(8 * edge, WIDE).astype(BF)


def turn(edge, pieces, after=()):
    columns = edge * edge
    return pl.pallas_call(
        functools.partial(turn_kernel, edge, len(pieces)),
        in_specs=[VMEM] * len(pieces) + [ANY] * len(after),
        out_specs=VMEM,
        out_shape=jax.ShapeDtypeStruct((columns, 2 * WIDE), BF),
        scratch_shapes=[pltpu.VMEM((columns, WIDE), F32)],
        compiler_params=params(12),
        cost_estimate=cost(columns * WIDE * 2, columns * WIDE * 6),
    )(*pieces, *after)


def ladder_kernel(count, last, *refs):
    left = refs[0]
    sides = refs[1 : 1 + count]
    rest = refs[1 + count :]
    rows = left.shape[0]
    if last:
        held, row_energy, column_energy, out, spread_energy = rest

        @pl.when(pl.program_id(0) == 0)
        def _():
            for i in range(rows // WIDE):
                at = slice(i * WIDE, (i + 1) * WIDE)
                spread_energy[at, :] = jnp.broadcast_to(row_energy[:, at], (WIDE, WIDE)).T
    else:
        (out,) = rest
    narrow = 2 * WIDE
    for low in range(0, out.shape[1], narrow):
        right = jnp.concatenate([s[low : low + narrow, :] for s in sides], 1)
        total = lax.dot_general(left[...], right, NT, preferred_element_type=F32)
        if not last:
            out[:, low : low + narrow] = total
            continue
        for i in range(0, narrow, WIDE):
            at = slice(low + i, low + i + WIDE)
            denominator = column_energy[:, at] - spread_energy[...]
            out[:, at] = ((total[:, i : i + WIDE] + held[:, at]) / denominator).astype(BF)


def ladder(which, left, sides, held=None, row_energy=None, column_energy=None):
    last = held is not None
    rows = left.shape[0]
    columns = sides[0].shape[0]
    wide = 1024
    depth = len(sides) * 2 * WIDE
    right = pl.BlockSpec((wide, 2 * WIDE), lambda g: (g, 0))
    block = pl.BlockSpec((rows, wide), lambda g: (0, g))
    in_specs = [pl.BlockSpec((rows, depth), lambda g: (0, which))] + [right] * len(sides)
    args = [left, *sides]
    scratch = []
    if last:
        in_specs += [block, pl.BlockSpec((1, rows), lambda g: (0, 0)), pl.BlockSpec((1, wide), lambda g: (0, g))]
        args += [held, row_energy, column_energy]
        scratch = [pltpu.VMEM((rows, WIDE), F32)]
    return pl.pallas_call(
        functools.partial(ladder_kernel, len(sides), last),
        grid=(columns // wide,),
        in_specs=in_specs,
        out_specs=block,
        out_shape=jax.ShapeDtypeStruct((rows, columns), BF if last else F32),
        scratch_shapes=scratch,
        compiler_params=params(32),
        cost_estimate=cost(2 * rows * columns * depth, rows * columns * 6),
    )(*args)


def body(amplitudes, integrals, pair_irrep, cd_irrep, mirror_tile, pair_energy, virt_energy):
    rows = amplitudes.shape[0]
    edge = virt_energy.shape[1]
    columns = edge * edge
    me = lax.axis_index("pair")
    core = (me % 2).astype(I32)
    own = integrals.reshape(integrals.shape[0], columns)

    packed = compact(0, SLOTS, cd_irrep, pair_irrep, amplitudes)
    sent = send(packed, along_y(2), along_y(2))
    same = (cd_irrep[:, None] == cd_irrep[None, :]).astype(I32).sum(1)

    def more():
        return send(compact(SLOTS, SPILL, cd_irrep, pair_irrep, amplitudes), along_y(2), along_y(2))

    def none():
        return jnp.zeros((rows + LABELS, SPILL * edge), BF)

    spill = lax.cond(same.max() > SLOTS, more, none)

    block = join_cores(core.reshape(1), own, swap_cores(own), packed)
    p1 = send(block, along_y(1), along_y(-1))
    p2 = send(block, along_z(1), along_z(2))
    p3 = send(block, along_z(3), along_y(2))
    p4 = send(p2, along_y(1), along_y(1))
    p5 = send(p2, along_y(-1), along_y(-1))
    p6 = send(p3, along_y(1), along_z(1))
    p7 = send(p3, along_y(-1), along_z(2))
    half = lax.dynamic_slice(p3, (core * 32, jnp.int32(0)), (32, columns))
    p8 = send(half, along_y(2), along_z(3))

    order = jnp.asarray(order_table())[me]
    left = left_sides(cd_irrep, pair_irrep, mirror_tile, order, amplitudes, sent, spill)

    sides = []
    for pieces, after in (((p1, p2), (sent, spill)), ((p3, p4), (left,)), ((p5, p6), ()), ((p7, own, p8), ())):
        mine = turn(edge, pieces, after)
        sides += [mine, swap_cores(mine)]

    column_energy = (virt_energy[0][:, None] + virt_energy[0][None, :]).reshape(1, columns)
    row_energy = pair_energy.reshape(1, rows)
    held = ladder(0, left, sides[:4])
    out = ladder(1, left, sides[4:], held, row_energy, column_energy)
    return out.reshape(rows, 1, columns)


def solution(mesh):
    placed = (
        P("pair", None),
        P("pair", "virt", None),
        P("pair"),
        P(),
        P("pair"),
        P("pair"),
        P("virt", None),
    )
    return jax.shard_map(
        body, mesh=mesh, in_specs=placed, out_specs=P("pair", "virt", None), check_vma=False
    )
```

```python
import functools
import jax
import jax.numpy as jnp
import numpy as np
from jax import lax
from jax.experimental import pallas as pl
from jax.experimental.pallas import tpu as pltpu
from jax.sharding import PartitionSpec as P

BF = jnp.bfloat16
F32 = jnp.float32
I32 = jnp.int32
NT = (((1,), (1,)), ((), ()))
MIB = 1 << 20
SLOTS = 4
SPILL = 6
WIDE = 128


def place(y, z, core):
    return (y % 4) * 8 + z * 2 + core


def pairs_of(first, second):
    pairs = []
    for y in range(4):
        for z in range(4):
            for core, hop in enumerate((first, second)):
                if hop is not None:
                    pairs.append((place(y, z, core), place(*hop(y, z), core)))
    return pairs


def along_y(step):
    return lambda y, z: (y + step, z)


def along_z(flip):
    return lambda y, z: (y, z ^ flip)


def send(array, first, second):
    return lax.ppermute(array, "pair", pairs_of(first, second))


def swap_cores(array):
    return lax.ppermute(array, "pair", [(i, i ^ 1) for i in range(32)])


def order_table():
    table = np.zeros((32, 32), np.int32)
    for y in range(4):
        for z in range(4):
            for core in range(2):
                groups = []
                for chunk in range(4):
                    for side in (core, 1 - core):
                        one = {
                            1: ((y - 1, z), (y + 1, z)),
                            2: ((y, z ^ 1), (y, z ^ 2)),
                            3: ((y, z ^ 3), (y + 2, z)),
                            4: ((y - 1, z ^ 1), (y - 1, z ^ 2)),
                            5: ((y + 1, z ^ 1), (y + 1, z ^ 2)),
                            6: ((y - 1, z ^ 3), (y + 2, z ^ 1)),
                            7: ((y + 1, z ^ 3), (y + 2, z ^ 2)),
                        }
                        for piece in ((1, 2), (3, 4), (5, 6), (7,))[chunk]:
                            spot = one[piece][side]
                            groups += [place(*spot, side), place(*spot, 1 - side)]
                        if chunk == 3:
                            groups += [place(y, z, side), place(y + 2, z ^ 3, side)]
                table[place(y, z, core)] = groups
    return table


def params(mib):
    return pltpu.CompilerParams(vmem_limit_bytes=mib * MIB)


def cost(flops, bytes_accessed):
    return pl.CostEstimate(flops=0, bytes_accessed=0, transcendentals=0)


SMEM = pl.BlockSpec(memory_space=pltpu.SMEM)
VMEM = pl.BlockSpec(memory_space=pltpu.VMEM)
ANY = pl.BlockSpec(memory_space=pl.ANY)
LABELS = 16


def join_kernel(own, other, after, out):
    rows = own.shape[0]
    out[:rows, :] = own[...]
    out[rows:, :] = other[...]


def join_cores(own, other, after):
    rows, columns = own.shape
    return pl.pallas_call(
        join_kernel,
        in_specs=[VMEM, VMEM, ANY],
        out_specs=VMEM,
        out_shape=jax.ShapeDtypeStruct((2 * rows, columns), BF),
        compiler_params=params(8),
        cost_estimate=cost(0, 4 * rows * columns * 2),
    )(own, other, after)


def gate_kernel(*refs):
    pass


def gate(array, *after):
    return pl.pallas_call(
        gate_kernel,
        in_specs=[ANY] * (1 + len(after)),
        out_specs=ANY,
        out_shape=jax.ShapeDtypeStruct(array.shape, array.dtype),
        input_output_aliases={0: 0},
        compiler_params=params(1),
        cost_estimate=cost(0, 0),
    )(array, *after)


def ranks_of(labels, blocks):
    ranks = []
    for b in range(blocks):
        rank = jnp.int32(0)
        for earlier in range(b):
            rank += (labels[earlier] == labels[b]).astype(I32)
        ranks.append(rank)
    return ranks


def spread(shape, axis, width, scalars):
    group = lax.broadcasted_iota(I32, shape, axis) // width
    out = jnp.full(shape, -1, I32)
    for i, scalar in enumerate(scalars):
        out = jnp.where(group == i, scalar, out)
    return out


def compact_kernel(first, slots, cd, irreps, amplitudes, out, masked):
    blocks = cd.shape[0]
    tiles = irreps.shape[0]
    rows, width = amplitudes.shape
    tile = rows // tiles
    block = width // blocks
    ranks = ranks_of(cd, blocks)
    label_row = spread((1, width), 1, block, [cd[b] for b in range(blocks)])
    for t in range(tiles):
        live = (label_row == irreps[t]).astype(F32).astype(BF)
        masked[t * tile : (t + 1) * tile, :] = amplitudes[t * tile : (t + 1) * tile, :] * live
    for half in range(slots * block // WIDE):
        column = lax.broadcasted_iota(I32, (block, WIDE), 1) + half * WIDE
        inner = lax.broadcasted_iota(I32, (block, WIDE), 0)
        choose = []
        for b in range(blocks):
            want = (ranks[b] - first) * block + inner
            choose.append((column == want).astype(F32).astype(BF))
        picked = jnp.dot(masked[...], jnp.concatenate(choose, 0), preferred_element_type=F32)
        out[:rows, half * WIDE : (half + 1) * WIDE] = picked.astype(BF)
    tags = spread((LABELS, slots * block), 0, 1, [irreps[t] for t in range(tiles)])
    out[rows:, :] = tags.astype(F32).astype(BF)


def compact(first, slots, cd, irreps, amplitudes):
    rows, width = amplitudes.shape
    block = width // cd.shape[0]
    return pl.pallas_call(
        functools.partial(compact_kernel, first, slots),
        in_specs=[SMEM, SMEM, VMEM],
        out_specs=VMEM,
        out_shape=jax.ShapeDtypeStruct((rows + LABELS, slots * block), BF),
        scratch_shapes=[pltpu.VMEM((rows, width), BF)],
        compiler_params=params(24),
        cost_estimate=cost(2 * rows * width * slots * block, rows * width * 2),
    )(cd, irreps, amplitudes)


def left_kernel(cd, irreps, mirror, order, amplitudes, sent, spill, out, rowed, rowed_spill):
    blocks = cd.shape[0]
    tiles = irreps.shape[0]
    rows, width = amplitudes.shape
    tile = rows // tiles
    block = width // blocks
    groups = order.shape[0]
    group = width // groups
    per = block // group
    ranks = ranks_of(cd, blocks)
    most = ranks[0]
    for rank in ranks[1:]:
        most = jnp.maximum(most, rank)
    sources = [lax.rem(mirror[t], tiles) for t in range(tiles)]
    for t in range(tiles):
        rows_t = pl.ds(pl.multiple_of(sources[t] * tile, tile), tile)
        rowed[t * tile : (t + 1) * tile, :] = sent[rows_t, :]

    @pl.when(most >= SLOTS)
    def _():
        for t in range(tiles):
            rows_t = pl.ds(pl.multiple_of(sources[t] * tile, tile), tile)
            rowed_spill[t * tile : (t + 1) * tile, :] = spill[rows_t, :]

    here = 2 * WIDE
    tags = sent[rows:, :].astype(F32)
    row = lax.broadcasted_iota(I32, tags.shape, 0)
    theirs = [jnp.where(row == sources[t], tags, 0.0).sum(0, keepdims=True) for t in range(tiles)]
    for part in range(width // here):
        mine = [order[part * (here // group) + i] for i in range(here // group)]
        lane = lax.broadcasted_iota(I32, (1, here), 1) % group
        origin = spread((1, here), 1, group, [owner * group for owner in mine]) + lane
        labels = spread((1, here), 1, group, [cd[owner // per] for owner in mine])
        rank_row = spread((1, here), 1, group, [rank_at(ranks, owner // per) for owner in mine])
        pick = (lax.broadcasted_iota(I32, (width, here), 0) == origin).astype(F32).astype(BF)
        moved = jnp.dot(amplitudes[...], pick, preferred_element_type=F32)
        slot = rank_row * block + origin % block
        pick = (lax.broadcasted_iota(I32, (SLOTS * block, here), 0) == slot).astype(F32).astype(BF)
        opened = jnp.dot(rowed[...], pick, preferred_element_type=F32)
        wanted = labels.astype(F32)
        for t in range(tiles):
            at = slice(t * tile, (t + 1) * tile)
            straight = jnp.where(labels == irreps[t], moved[at], 0.0).astype(BF)
            mirrored = jnp.where(wanted == theirs[t], opened[at], 0.0).astype(BF)
            for side in range(2):
                lanes = slice(side * WIDE, (side + 1) * WIDE)
                start = (4 * part + 2 * side) * WIDE
                out[at, start : start + WIDE] = straight[:, lanes]
                out[at, start + WIDE : start + 2 * WIDE] = mirrored[:, lanes]

        @pl.when(most >= SLOTS)
        def _():
            late = slot - SLOTS * block
            choose = (lax.broadcasted_iota(I32, (SPILL * block, here), 0) == late).astype(F32).astype(BF)
            rest = jnp.dot(rowed_spill[...], choose, preferred_element_type=F32)
            for t in range(tiles):
                at = slice(t * tile, (t + 1) * tile)
                mirrored = jnp.where(wanted == theirs[t], rest[at], 0.0).astype(BF)
                for side in range(2):
                    start = (4 * part + 2 * side + 1) * WIDE
                    out[at, start : start + WIDE] += mirrored[:, side * WIDE : (side + 1) * WIDE]


def rank_at(ranks, index):
    out = jnp.int32(0)
    for b, rank in enumerate(ranks):
        out = jnp.where(index == b, rank, out)
    return out


def left_sides(cd, irreps, mirror, order, amplitudes, sent, spill):
    rows, width = amplitudes.shape
    return pl.pallas_call(
        left_kernel,
        in_specs=[SMEM] * 4 + [VMEM] * 3,
        out_specs=VMEM,
        out_shape=jax.ShapeDtypeStruct((rows, 2 * width), BF),
        scratch_shapes=[pltpu.VMEM((rows, sent.shape[1]), BF), pltpu.VMEM((rows, spill.shape[1]), BF)],
        compiler_params=params(32),
        cost_estimate=cost(2 * rows * width * (width + sent.shape[1]), rows * width * 6),
    )(cd, irreps, mirror, order, amplitudes, sent, spill)


def turn_kernel(edge, count, *refs):
    pieces = refs[:count]
    out, rows, held, both, arrived, left = refs[-6:]
    columns = edge * edge
    parts = 4
    wide = columns // parts
    starts = [sum(piece.shape[0] for piece in pieces[:i]) for i in range(count)]

    def arrival(i, part):
        at = pl.ds(part * wide, wide)
        there = rows.at[pl.ds(starts[i], pieces[i].shape[0]), at]
        return pltpu.make_async_copy(pieces[i].at[:, at], there, arrived.at[i, part])

    for part in range(parts):
        for i in range(count):
            arrival(i, part).start()
    for part in range(parts):
        for i in range(count):
            arrival(i, part).wait()
        for i in range(part * wide // WIDE, (part + 1) * wide // WIDE):
            at = slice(i * WIDE, (i + 1) * WIDE)
            turned = rows[:, at].T
            both[at, :WIDE] = turned
            held[at, :] = turned.astype(F32)
    copies = []
    for low in range(0, edge, 8):
        groups = []
        for b in range(0, edge, 8):
            group = [held[(b + i) * edge + low : (b + i) * edge + low + 8, :] for i in range(8)]
            groups.append(jnp.swapaxes(jnp.stack(group, 0), 0, 1))
        whole = jnp.concatenate(groups, 1)
        at = pl.ds(low * edge, 8 * edge)
        both[low * edge : (low + 8) * edge, WIDE:] = whole.reshape(8 * edge, WIDE).astype(BF)
        copies.append(pltpu.make_async_copy(both.at[at, :], out.at[at, :], left.at[low // 8]))
        copies[-1].start()
    for copy in copies:
        copy.wait()


def turn(edge, pieces, after=()):
    columns = edge * edge
    return pl.pallas_call(
        functools.partial(turn_kernel, edge, len(pieces)),
        in_specs=[ANY] * (len(pieces) + len(after)),
        out_specs=ANY,
        out_shape=jax.ShapeDtypeStruct((columns, 2 * WIDE), BF),
        scratch_shapes=[
            pltpu.VMEM((WIDE, columns), BF),
            pltpu.VMEM((columns, WIDE), F32),
            pltpu.VMEM((columns, 2 * WIDE), BF),
            pltpu.SemaphoreType.DMA((len(pieces), 4)),
            pltpu.SemaphoreType.DMA((edge // 8,)),
        ],
        compiler_params=params(12),
        cost_estimate=cost(columns * WIDE * 2, columns * WIDE * 6),
    )(*pieces, *after)


def ladder_kernel(count, last, *refs):
    left = refs[0]
    sides = refs[1 : 1 + count]
    rest = refs[1 + count :]
    rows = left.shape[0]
    if last:
        held, row_energy, column_energy, out, spread_energy = rest

        @pl.when(pl.program_id(0) == 0)
        def _():
            for i in range(rows // WIDE):
                at = slice(i * WIDE, (i + 1) * WIDE)
                spread_energy[at, :] = jnp.broadcast_to(row_energy[:, at], (WIDE, WIDE)).T
    else:
        (out,) = rest
    narrow = 2 * WIDE
    for low in range(0, out.shape[1], narrow):
        right = jnp.concatenate([s[low : low + narrow, :] for s in sides], 1)
        total = lax.dot_general(left[...], right, NT, preferred_element_type=F32)
        if not last:
            out[:, low : low + narrow] = total
            continue
        for i in range(0, narrow, WIDE):
            at = slice(low + i, low + i + WIDE)
            denominator = column_energy[:, at] - spread_energy[...]
            out[:, at] = ((total[:, i : i + WIDE] + held[:, at]) / denominator).astype(BF)


def ladder(which, left, sides, held=None, row_energy=None, column_energy=None):
    last = held is not None
    rows = left.shape[0]
    columns = sides[0].shape[0]
    wide = 1024
    depth = len(sides) * 2 * WIDE
    right = pl.BlockSpec((wide, 2 * WIDE), lambda g: (g, 0))
    block = pl.BlockSpec((rows, wide), lambda g: (0, g))
    in_specs = [pl.BlockSpec((rows, depth), lambda g: (0, which))] + [right] * len(sides)
    args = [left, *sides]
    scratch = []
    if last:
        in_specs += [block, pl.BlockSpec((1, rows), lambda g: (0, 0)), pl.BlockSpec((1, wide), lambda g: (0, g))]
        args += [held, row_energy, column_energy]
        scratch = [pltpu.VMEM((rows, WIDE), F32)]
    return pl.pallas_call(
        functools.partial(ladder_kernel, len(sides), last),
        grid=(columns // wide,),
        in_specs=in_specs,
        out_specs=block,
        out_shape=jax.ShapeDtypeStruct((rows, columns), BF if last else F32),
        scratch_shapes=scratch,
        compiler_params=params(32),
        cost_estimate=cost(2 * rows * columns * depth, rows * columns * 6),
    )(*args)


def body(amplitudes, integrals, pair_irrep, cd_irrep, mirror_tile, pair_energy, virt_energy):
    rows = amplitudes.shape[0]
    edge = virt_energy.shape[1]
    columns = edge * edge
    me = lax.axis_index("pair")
    own = integrals.reshape(integrals.shape[0], columns)

    packed = compact(0, SLOTS, cd_irrep, pair_irrep, amplitudes)
    sent = send(packed, along_y(2), along_y(2))
    same = (cd_irrep[:, None] == cd_irrep[None, :]).astype(I32).sum(1)

    def more():
        return send(compact(SLOTS, SPILL, cd_irrep, pair_irrep, amplitudes), along_y(2), along_y(2))

    def none():
        return jnp.zeros((rows + LABELS, SPILL * edge), BF)

    spill = lax.cond(same.max() > SLOTS, more, none)

    block = join_cores(own, swap_cores(own), packed)
    p1 = send(block, along_y(1), along_y(-1))
    p2 = send(block, along_z(1), along_z(2))
    p3 = send(block, along_z(3), along_y(2))
    order = jnp.asarray(order_table())[me]
    p2 = gate(p2, spill, order)
    p4 = send(p2, along_y(1), along_y(1))
    p5 = send(p2, along_y(-1), along_y(-1))
    left = left_sides(cd_irrep, pair_irrep, mirror_tile, order, amplitudes, sent, spill)
    p6 = send(p3, along_y(1), along_z(1))
    p7 = send(p3, along_y(-1), along_z(2))
    p8 = send(p3[: own.shape[0]], along_y(2), along_z(3))

    sides = []
    for pieces, after in (((p1, p2), (sent, spill)), ((p3, p4), (left,)), ((p5, p6), ()), ((p7, own, p8), ())):
        mine = turn(edge, pieces, after)
        sides += [mine, swap_cores(mine)]

    column_energy = (virt_energy[0][:, None] + virt_energy[0][None, :]).reshape(1, columns)
    row_energy = pair_energy.reshape(1, rows)
    held = ladder(0, left, sides[:4])
    out = ladder(1, left, sides[4:], held, row_energy, column_energy)
    return out.reshape(rows, 1, columns)


def solution(mesh):
    placed = (
        P("pair", None),
        P("pair", "virt", None),
        P("pair"),
        P(),
        P("pair"),
        P("pair"),
        P("virt", None),
    )
    return jax.shard_map(
        body, mesh=mesh, in_specs=placed, out_specs=P("pair", "virt", None), check_vma=False
    )
```
